32 devices in a mesh: seq: 4 (over y, x), fsdp: 8 (over z, core).
Axes of the slice: x: 2, y: 2, z: 4, core: 2. Of those that a mesh axis runs over, the one named last changes fastest.
Arguments:
- hidden_in: bfloat16 [8, 2048, 768], P('fsdp', 'seq'), may hold values from -6 to 6
- norm_gain: float32 [768], replicated, may hold values from 0.5 to 1.5
- w_in: bfloat16 [768, 3352], P('fsdp'), may hold values from -0.21875 to 0.21875
- conv_weight: float32 [4, 1792], replicated, may hold values from -3 to 3
- conv_bias: float32 [1792], replicated, may hold values from -1.5 to 1.5
- dt_bias: float32 [24], replicated, may hold values from -4 to -1
- a_log: float32 [24], replicated, may hold values from -4 to 2.8
- skip_gain: float32 [24], replicated, may hold values from 0.1 to 1
- gate_gain: float32 [1536], replicated, may hold values from 0.5 to 1.5
- w_out: bfloat16 [1536, 768], P('fsdp'), may hold values from -0.15625 to 0.15625
- cotangent: bfloat16 [8, 2048, 768], P('fsdp', 'seq'), may hold values from -6 to 6
Outputs:
- layer_out: bfloat16 [8, 2048, 768], P('fsdp', 'seq')
- d_hidden: float32 [8, 2048, 768], P('fsdp', 'seq')
- d_norm_gain: float32 [768], replicated
- d_w_in: float32 [768, 3352], P('fsdp')
- d_conv_weight: float32 [4, 1792], replicated
- d_conv_bias: float32 [1792], replicated
- d_dt_bias: float32 [24], replicated
- d_a_log: float32 [24], replicated
- d_skip_gain: float32 [24], replicated
- d_gate_gain: float32 [1536], replicated
- d_w_out: float32 [1536, 768], P('fsdp')
The draws below stay inside these ranges and needn't reach their ends.
All inputs are finite; a program needn't handle non-finite values.
Results may differ from the reference program's by a relative error of at most 0.012.
Values may be sent and summed in bfloat16 or wider, within the bound.
A program may use at most 128 MiB of HBM per device.

```python
import jax
import jax.numpy as jnp
from jax import lax

D = 768
HEADS = 24
HEAD_DIM = 64
STATE = 128
CONVW = 4
SPAN = 256
INNER = 1536
CONV = 1792
PROJ = 3352
LEN = 2048
BATCH = 8


def level_of(own_key, extent, shards, low, top_value):
    loudness = 1.0
    for axis_at, blocks in shards:
        draws = jax.random.uniform(jax.random.fold_in(jax.random.fold_in(own_key, 6), axis_at), (blocks,), jnp.float32, low / len(shards), top_value / len(shards))
        loudness = loudness * jnp.repeat(jnp.exp(draws), extent[axis_at] // blocks).reshape((-1,) + (1,) * (len(extent) - 1 - axis_at))
    return loudness


def centred(own_key, shape, scale, limit, cuts=(), kind=jnp.bfloat16):
    values = scale * jax.random.normal(own_key, shape, jnp.float32)
    if cuts:
        values = values * level_of(own_key, shape, cuts, -0.22, 0.18)
    return jnp.clip(values, -limit, limit).astype(kind)


def setup_inputs(seed: int = 0) -> dict:
    seeds = jax.random.split(jax.random.key(seed), 12)
    return {
        "hidden_in": centred(seeds[0], (BATCH, LEN, D), 1.0, 6.0, ((0, 8), (1, 4))),
        "norm_gain": jnp.clip(1.0 + 0.1 * jax.random.normal(seeds[1], (D,), jnp.float32), 0.5, 1.5),
        "w_in": centred(seeds[2], (D, PROJ), D ** -0.5, 0.21875, ((0, 8),)),
        "conv_weight": centred(seeds[3], (CONVW, CONV), CONVW ** -0.5, 3.0, (), jnp.float32),
        "conv_bias": centred(seeds[4], (CONV,), 0.3, 1.5, (), jnp.float32),
        "dt_bias": jnp.clip(jax.random.uniform(seeds[5], (HEADS,), jnp.float32, -4.0, -1.0), -4.0, -1.0),
        "a_log": jnp.clip(jax.random.uniform(seeds[6], (HEADS,), jnp.float32, -4.0, 2.8), -4.0, 2.8),
        "skip_gain": jnp.clip(jax.random.uniform(seeds[7], (HEADS,), jnp.float32, 0.1, 1.0), 0.1, 1.0),
        "gate_gain": jnp.clip(1.0 + 0.1 * jax.random.normal(seeds[8], (INNER,), jnp.float32), 0.5, 1.5),
        "w_out": centred(seeds[9], (INNER, D), INNER ** -0.5, 0.15625, ((0, 8),)),
        "cotangent": centred(seeds[10], (BATCH, LEN, D), 1.0, 6.0, ((0, 8), (1, 4))),
    }


epsilon = 1e-05
precise = lax.Precision.HIGHEST

@jax.custom_vjp
def low(v):
    return lax.optimization_barrier(v.astype(jnp.bfloat16)).astype(jnp.float32)

@jax.custom_vjp
def low_back(v):
    return v

def low_keep(v):
    return (low(v), None)

def low_pass(kept, grad):
    return (grad,)

def back_keep(v):
    return (v, None)

def back_low(kept, grad):
    return (low(grad),)
low.defvjp(low_keep, low_pass)
low_back.defvjp(back_keep, back_low)

def causal_conv(values, kernel):
    length = values.shape[0]
    padded = jnp.pad(values, ((CONVW - 1, 0), (0, 0)))
    summed = kernel[0] * padded[0:length]
    for offset in range(1, CONVW):
        summed = summed + kernel[offset] * padded[offset:offset + length]
    return summed

def state_scan(values, b_rows, c_rows, step_size, decay_rates):
    length, head_count, head_dim = values.shape
    block_count = length // SPAN
    causal_mask = jnp.arange(SPAN)[:, None] >= jnp.arange(SPAN)[None, :]

    def block_step(carried, pieces):
        x_block, b_block, c_block, dt_block = pieces
        decay_sum = jnp.cumsum(dt_block * decay_rates[None, :], axis=0)
        decay_cols = decay_sum.T
        intersection = jnp.dot(c_block, b_block.T, precision=precise)
        spread = jnp.where(causal_mask[None], decay_cols[:, :, None] - decay_cols[:, None, :], 0.0)
        factor = jnp.where(causal_mask[None], jnp.exp(spread), 0.0)
        mixing = factor * intersection[None] * dt_block.T[:, None, :]
        within = jnp.einsum('hts,shp->thp', mixing, x_block, precision=precise)
        earlier = jnp.einsum('tn,hpn->thp', c_block, carried, precision=precise) * jnp.exp(decay_sum)[:, :, None]
        remain = jnp.exp(decay_sum[-1][None, :] - decay_sum) * dt_block
        renewed = carried * jnp.exp(decay_sum[-1])[:, None, None] + jnp.einsum('sh,shp,sn->hpn', remain, x_block, b_block, precision=precise)
        return (renewed, within + earlier)
    initial = jnp.zeros((head_count, head_dim, b_rows.shape[1]), values.dtype)
    blocks = (values.reshape(block_count, SPAN, head_count, head_dim), b_rows.reshape(block_count, SPAN, b_rows.shape[1]), c_rows.reshape(block_count, SPAN, c_rows.shape[1]), step_size.reshape(block_count, SPAN, head_count))
    final_state, outputs = lax.scan(jax.checkpoint(block_step), initial, blocks)
    return outputs.reshape(length, head_count, head_dim)

def mixer_local(x_in, bc_in, dt_in, conv_x, conv_bc, bias_x, bias_bc, dt_shift, a_decay, skip_vals):
    length = x_in.shape[0]
    head_count = dt_in.shape[1]
    x_conv = jax.nn.silu(causal_conv(x_in, conv_x) + bias_x)
    bc_conv = jax.nn.silu(causal_conv(bc_in, conv_bc) + bias_bc)
    step_size = jax.nn.softplus(dt_in + dt_shift)
    decay_rates = -jnp.exp(a_decay)
    values = x_conv.reshape(length, head_count, HEAD_DIM)
    scanned = state_scan(values, bc_conv[:, :STATE], bc_conv[:, STATE:], step_size, decay_rates)
    return (scanned + skip_vals[None, :, None] * values).reshape(length, head_count * HEAD_DIM)

def layer_forward(hidden, norm_gain, w_in, conv_weight, conv_bias, dt_bias, a_log, skip_gain, gate_gain, w_out):

    def one_sequence(tokens):
        inv_rms = lax.rsqrt(lax.optimization_barrier(jnp.mean(tokens * tokens, axis=1, keepdims=True)) + epsilon)
        normed_in = low(tokens * inv_rms * norm_gain)
        projected = low_back(low(jnp.dot(normed_in, w_in, precision=precise)))
        gate_vals = projected[:, :INNER]
        x_vals = projected[:, INNER:2 * INNER]
        bc_vals = projected[:, 2 * INNER:2 * INNER + 2 * STATE]
        dt_vals = projected[:, 2 * INNER + 2 * STATE:]
        mixed_raw = mixer_local(x_vals, bc_vals, dt_vals, conv_weight[:, :INNER], conv_weight[:, INNER:], conv_bias[:INNER], conv_bias[INNER:], dt_bias, a_log, skip_gain)
        mixed_raw = low_back(low(mixed_raw))
        gated_vals = mixed_raw * jax.nn.silu(gate_vals)
        gate_rms = lax.rsqrt(lax.optimization_barrier(jnp.mean(gated_vals * gated_vals, axis=1, keepdims=True)) + epsilon)
        normed_out = low_back(low(gated_vals * gate_rms * gate_gain))
        return tokens + jnp.dot(normed_out, w_out, precision=precise)
    return lax.map(jax.checkpoint(one_sequence), hidden)

def reference(hidden_in, norm_gain, w_in, conv_weight, conv_bias, dt_bias, a_log, skip_gain, gate_gain, w_out, cotangent):
    layer_out, pullback = jax.vjp(layer_forward, hidden_in.astype(jnp.float32), norm_gain, w_in.astype(jnp.float32), conv_weight, conv_bias, dt_bias, a_log, skip_gain, gate_gain, w_out.astype(jnp.float32))
    gradients = pullback(cotangent.astype(jnp.float32))
    return (layer_out.astype(jnp.bfloat16), gradients[0], gradients[1], gradients[2], gradients[3], gradients[4], gradients[5], gradients[6], gradients[7], gradients[8], gradients[9])
```

```python
from functools import partial

import jax
import jax.numpy as jnp
from jax import lax
from jax.sharding import PartitionSpec as P

D = 768
HEADS = 24
HEAD_DIM = 64
STATE = 128
CONVW = 4
CHUNK = 128
INNER = 1536
CONV = INNER + 2 * STATE

epsilon = 1e-05
precise = lax.Precision.HIGHEST
bf16 = jnp.bfloat16
f32 = jnp.float32


@partial(jax.custom_vjp, nondiff_argnums=(0,))
def mm(spec, left, right):
    return jnp.einsum(spec, left.astype(bf16), right.astype(bf16), preferred_element_type=f32)


def mm_keep(spec, left, right):
    left, right = left.astype(bf16), right.astype(bf16)
    return jnp.einsum(spec, left, right, preferred_element_type=f32), (left, right)


def mm_back(spec, kept, grad):
    left, right = kept
    sides, out = spec.split("->")
    one, two = sides.split(",")
    grad = grad.astype(bf16)
    return (
        jnp.einsum(f"{out},{two}->{one}", grad, right, preferred_element_type=f32),
        jnp.einsum(f"{one},{out}->{two}", left, grad, preferred_element_type=f32),
    )


mm.defvjp(mm_keep, mm_back)


def over_heads(values):
    spread = jnp.repeat(jnp.eye(HEADS, dtype=f32), HEAD_DIM, axis=1)
    return jnp.einsum("...h,hk->...k", values, spread, precision=precise)


def shifted(values, by):
    count = lax.axis_size("seq")
    return lax.ppermute(values, "seq", [(at, at + by) for at in range(count - by)])


def incoming(final_state, total):
    sent = final_state.astype(bf16)
    result = shifted(sent, 1).astype(f32)
    gap = 0.0
    for by in range(2, lax.axis_size("seq")):
        gap = gap + shifted(total, by - 1)
        result = result + over_heads(jnp.exp(gap))[None, :] * shifted(sent, by).astype(f32)
    return result


def state_scan(values, b_rows, c_rows, step_size, decay_rates):
    length = values.shape[0]
    chunks = length // CHUNK
    causal = jnp.arange(CHUNK)[:, None] >= jnp.arange(CHUNK)[None, :]
    x_c = values.reshape(chunks, CHUNK, INNER)
    b_c = b_rows.reshape(chunks, CHUNK, STATE)
    c_c = c_rows.reshape(chunks, CHUNK, STATE)
    dt_c = step_size.reshape(chunks, CHUNK, HEADS)
    decay_sum = jnp.einsum(
        "ts,csh->cth", causal.astype(f32), dt_c * decay_rates, precision=precise
    )
    total = decay_sum[:, -1, :]
    remain = jnp.exp(total[:, None, :] - decay_sum) * dt_c
    gains = mm("csn,csk->cnk", b_c, x_c * over_heads(remain))
    whole = over_heads(jnp.exp(total))
    starts = [jnp.zeros((STATE, INNER), f32)]
    for at in range(chunks):
        starts.append(starts[-1] * whole[at][None, :] + gains[at])
    first = incoming(starts[-1], jnp.sum(total, axis=0))
    before = over_heads(jnp.exp(jnp.cumsum(total, axis=0) - total))
    begun = jnp.stack(starts[:-1]) + before[:, None, :] * first[None]
    decay_cols = jnp.swapaxes(decay_sum, 1, 2)
    spread = jnp.where(
        causal[None, None], decay_cols[:, :, :, None] - decay_cols[:, :, None, :], 0.0
    )
    factor = jnp.where(causal[None, None], jnp.exp(spread), 0.0)
    crossing = mm("ctn,csn->cts", c_c, b_c)
    mixing = factor * crossing[:, None] * jnp.swapaxes(dt_c, 1, 2)[:, :, None, :]
    within = mm("chts,chsp->chtp", mixing, jnp.swapaxes(x_c.reshape(chunks, CHUNK, HEADS, HEAD_DIM), 1, 2))
    within = jnp.swapaxes(within, 1, 2).reshape(chunks, CHUNK, INNER)
    earlier = mm("ctn,cnk->ctk", c_c, begun) * over_heads(jnp.exp(decay_sum))
    return (within + earlier).reshape(length, INNER)


def mixer_local(xbc, raw_step, conv_weight, conv_bias, dt_bias, a_log, skip_gain):
    length = xbc.shape[0]
    halo = shifted(xbc[length - CONVW + 1 :].astype(bf16), 1).astype(f32)
    padded = jnp.concatenate([halo, xbc], axis=0)
    summed = conv_bias[None, :]
    for at in range(CONVW):
        summed = summed + conv_weight[at] * padded[at : at + length]
    filtered = jax.nn.silu(summed)
    step_size = jax.nn.softplus(raw_step + dt_bias)
    values = filtered[:, :INNER]
    scanned = state_scan(
        values,
        filtered[:, INNER : INNER + STATE],
        filtered[:, INNER + STATE :],
        step_size,
        -jnp.exp(a_log),
    )
    return scanned + over_heads(skip_gain)[None, :] * values


def plain(left_mat, right_mat):
    return jnp.dot(left_mat, right_mat, preferred_element_type=f32)


def times_transposed(left_mat, right_mat):
    return lax.dot_general(
        left_mat, right_mat, (((1,), (1,)), ((), ())), preferred_element_type=f32
    )


def over_rows(left_mat, right_mat):
    return lax.dot_general(
        left_mat, right_mat, (((0,), (0,)), ((), ())), preferred_element_type=f32
    )


def gathered(rows):
    return lax.all_gather(rows, "fsdp", axis=0, tiled=True)


def reduced(part):
    rows = lax.psum_scatter(part.astype(bf16), "fsdp", scatter_dimension=0, tiled=True)
    return lax.psum(rows, "seq").astype(f32)


def body(
    hidden_in,
    norm_gain,
    w_in,
    conv_weight,
    conv_bias,
    dt_bias,
    a_log,
    skip_gain,
    gate_gain,
    w_out,
    cotangent,
):
    w_scan = gathered(w_in[:, INNER:])
    z_rows, o_rows, w_scan = lax.optimization_barrier((w_in[:, :INNER], w_out, w_scan))
    w_gate = gathered(z_rows)
    w_out_full = gathered(o_rows)
    tokens = hidden_in[0].astype(f32)
    inv_rms = lax.rsqrt(jnp.mean(tokens * tokens, axis=1, keepdims=True) + epsilon)
    normed_in = (tokens * inv_rms * norm_gain).astype(bf16)
    proj_scan = plain(normed_in, w_scan).astype(bf16)
    mixed_raw, mixer_back = jax.vjp(
        mixer_local,
        proj_scan[:, :CONV].astype(f32),
        proj_scan[:, CONV:].astype(f32),
        conv_weight,
        conv_bias,
        dt_bias,
        a_log,
        skip_gain,
    )
    gate_f = plain(normed_in, w_gate).astype(bf16).astype(f32)
    grad_out = cotangent[0]
    d_head = times_transposed(grad_out, w_out_full).astype(bf16).astype(f32)
    mixed_f = lax.optimization_barrier(mixed_raw.astype(bf16)).astype(f32)
    gate_sigmoid = jax.nn.sigmoid(gate_f)
    gate_silu = gate_f * gate_sigmoid
    gated_vals = mixed_f * gate_silu
    gate_rms = lax.rsqrt(jnp.mean(gated_vals * gated_vals, axis=1, keepdims=True) + epsilon)
    normed_out = (gated_vals * gate_rms * gate_gain).astype(bf16)
    d_w_out_part = over_rows(normed_out, grad_out)
    cross = jnp.mean(d_head * gate_gain * gated_vals, axis=1, keepdims=True)
    gain_grad = jnp.sum(d_head * gated_vals * gate_rms, axis=0)
    d_gated = gate_rms * gate_gain * d_head - gated_vals * gate_rms**3 * cross
    d_mixed = lax.optimization_barrier((d_gated * gate_silu).astype(bf16)).astype(f32)
    d_gate = (d_gated * mixed_f * gate_sigmoid * (1.0 + gate_f * (1.0 - gate_sigmoid))).astype(
        bf16
    )
    d_w_gate_part = over_rows(normed_in, d_gate)
    grad_w_out = reduced(d_w_out_part)
    grad_w_gate = reduced(d_w_gate_part)
    result = (tokens + plain(normed_out, w_out_full)).astype(bf16)
    d_xbc, d_step, conv_grad, bias_grad, shift_grad, decay_grad, skip_grad = mixer_back(d_mixed)
    d_scan = jnp.concatenate([d_xbc, d_step], axis=1).astype(bf16)
    grad_w_scan = reduced(over_rows(normed_in, d_scan))
    d_normed_in = times_transposed(d_gate, w_gate) + times_transposed(d_scan, w_scan)
    norm_gain_grad = jnp.sum(d_normed_in * tokens * inv_rms, axis=0)
    norm_cross = jnp.sum(d_normed_in * norm_gain * tokens, axis=1, keepdims=True)
    d_tokens = (
        inv_rms * norm_gain * d_normed_in
        - tokens * inv_rms**3 * norm_cross / D
        + grad_out.astype(f32)
    )
    small = (
        norm_gain_grad,
        conv_grad,
        bias_grad,
        shift_grad,
        decay_grad,
        skip_grad,
        gain_grad,
    )
    flat = lax.psum(jnp.concatenate([each.reshape(-1) for each in small]), ("seq", "fsdp"))
    sums, at = [], 0
    for each in small:
        sums.append(flat[at : at + each.size].reshape(each.shape))
        at += each.size
    return (
        result[None],
        d_tokens[None],
        sums[0],
        jnp.concatenate([grad_w_gate, grad_w_scan], axis=1),
        sums[1],
        sums[2],
        sums[3],
        sums[4],
        sums[5],
        sums[6],
        grad_w_out,
    )


def solution(mesh):
    rows = P("fsdp", None)
    part = P("fsdp", "seq", None)
    return jax.shard_map(
        body,
        mesh=mesh,
        in_specs=(part, P(), rows, P(), P(), P(), P(), P(), P(), rows, part),
        out_specs=(part, part, P(), rows, P(), P(), P(), P(), P(), P(), rows),
        check_vma=False,
    )
```

```python
from functools import partial

import jax
import jax.numpy as jnp
from jax import lax
from jax.sharding import PartitionSpec as P

D = 768
HEADS = 24
HEAD_DIM = 64
STATE = 128
CONVW = 4
CHUNK = 128
INNER = 1536
CONV = INNER + 2 * STATE

epsilon = 1e-05
precise = lax.Precision.HIGHEST
bf16 = jnp.bfloat16
f32 = jnp.float32


@partial(jax.custom_vjp, nondiff_argnums=(0,))
def mm(spec, left, right):
    return jnp.einsum(spec, left.astype(bf16), right.astype(bf16), preferred_element_type=f32)


def mm_keep(spec, left, right):
    left, right = left.astype(bf16), right.astype(bf16)
    return jnp.einsum(spec, left, right, preferred_element_type=f32), (left, right)


def mm_back(spec, kept, grad):
    left, right = kept
    sides, out = spec.split("->")
    one, two = sides.split(",")
    grad = grad.astype(bf16)
    return (
        jnp.einsum(f"{out},{two}->{one}", grad, right, preferred_element_type=f32),
        jnp.einsum(f"{one},{out}->{two}", left, grad, preferred_element_type=f32),
    )


mm.defvjp(mm_keep, mm_back)


def over_heads(values):
    spread = jnp.repeat(jnp.eye(HEADS, dtype=f32), HEAD_DIM, axis=1)
    return jnp.einsum("...h,hk->...k", values, spread, precision=precise)


def shifted(values, by):
    count = lax.axis_size("seq")
    return lax.ppermute(values, "seq", [(at, at + by) for at in range(count - by)])


def incoming(final_state, total):
    sent = final_state.astype(bf16)
    result = shifted(sent, 1).astype(f32)
    gap = 0.0
    for by in range(2, lax.axis_size("seq")):
        gap = gap + shifted(total, by - 1)
        result = result + over_heads(jnp.exp(gap))[None, :] * shifted(sent, by).astype(f32)
    return result


def state_scan(values, b_rows, c_rows, step_size, decay_rates):
    length = values.shape[0]
    chunks = length // CHUNK
    causal = jnp.arange(CHUNK)[:, None] >= jnp.arange(CHUNK)[None, :]
    x_c = values.reshape(chunks, CHUNK, INNER)
    b_c = b_rows.reshape(chunks, CHUNK, STATE)
    c_c = c_rows.reshape(chunks, CHUNK, STATE)
    dt_c = step_size.reshape(chunks, CHUNK, HEADS)
    decay_sum = jnp.einsum(
        "ts,csh->cth", causal.astype(f32), dt_c * decay_rates, precision=precise
    )
    total = decay_sum[:, -1, :]
    remain = jnp.exp(total[:, None, :] - decay_sum) * dt_c
    gains = mm("csn,csk->cnk", b_c, x_c * over_heads(remain))
    whole = over_heads(jnp.exp(total))
    starts = [jnp.zeros((STATE, INNER), f32)]
    for at in range(chunks):
        starts.append(starts[-1] * whole[at][None, :] + gains[at])
    first = incoming(starts[-1], jnp.sum(total, axis=0))
    before = over_heads(jnp.exp(jnp.cumsum(total, axis=0) - total))
    begun = jnp.stack(starts[:-1]) + before[:, None, :] * first[None]
    decay_cols = jnp.swapaxes(decay_sum, 1, 2)
    spread = jnp.where(
        causal[None, None], decay_cols[:, :, :, None] - decay_cols[:, :, None, :], 0.0
    )
    factor = jnp.where(causal[None, None], jnp.exp(spread), 0.0)
    crossing = mm("ctn,csn->cts", c_c, b_c)
    mixing = factor * crossing[:, None] * jnp.swapaxes(dt_c, 1, 2)[:, :, None, :]
    within = mm("chts,chsp->chtp", mixing, jnp.swapaxes(x_c.reshape(chunks, CHUNK, HEADS, HEAD_DIM), 1, 2))
    within = jnp.swapaxes(within, 1, 2).reshape(chunks, CHUNK, INNER)
    earlier = mm("ctn,cnk->ctk", c_c, begun) * over_heads(jnp.exp(decay_sum))
    return (within + earlier).reshape(length, INNER)


def mixer_local(xbc, raw_step, conv_weight, conv_bias, dt_bias, a_log, skip_gain):
    length = xbc.shape[0]
    halo = shifted(xbc[length - CONVW + 1 :].astype(bf16), 1).astype(f32)
    padded = jnp.concatenate([halo, xbc], axis=0)
    summed = conv_bias[None, :]
    for at in range(CONVW):
        summed = summed + conv_weight[at] * padded[at : at + length]
    filtered = jax.nn.silu(summed)
    step_size = jax.nn.softplus(raw_step + dt_bias)
    values = filtered[:, :INNER]
    scanned = state_scan(
        values,
        filtered[:, INNER : INNER + STATE],
        filtered[:, INNER + STATE :],
        step_size,
        -jnp.exp(a_log),
    )
    return scanned + over_heads(skip_gain)[None, :] * values


def plain(left_mat, right_mat):
    return jnp.dot(left_mat, right_mat, preferred_element_type=f32)


def times_transposed(left_mat, right_mat):
    return lax.dot_general(
        left_mat, right_mat, (((1,), (1,)), ((), ())), preferred_element_type=f32
    )


def over_rows(left_mat, right_mat):
    return lax.dot_general(
        left_mat, right_mat, (((0,), (0,)), ((), ())), preferred_element_type=f32
    )


def gathered(rows):
    return lax.all_gather(rows, "fsdp", axis=0, tiled=True)


def seq_total(rows):
    count = lax.axis_size("seq")
    terms = [rows.astype(f32)]
    for other in range(1, count):
        terms.append(lax.ppermute(rows, "seq", [(at, at ^ other) for at in range(count)]).astype(f32))
    while len(terms) > 1:
        terms = [one + two for one, two in zip(terms[::2], terms[1::2])]
    return terms[0]


def reduced(part):
    rows = lax.psum_scatter(part.astype(bf16), "fsdp", scatter_dimension=0, tiled=True)
    return seq_total(rows)


def body(
    hidden_in,
    norm_gain,
    w_in,
    conv_weight,
    conv_bias,
    dt_bias,
    a_log,
    skip_gain,
    gate_gain,
    w_out,
    cotangent,
):
    w_scan = gathered(w_in[:, INNER:])
    z_rows, o_rows, w_scan = lax.optimization_barrier((w_in[:, :INNER], w_out, w_scan))
    w_gate = gathered(z_rows)
    w_out_full = gathered(o_rows)
    tokens = hidden_in[0].astype(f32)
    inv_rms = lax.rsqrt(jnp.mean(tokens * tokens, axis=1, keepdims=True) + epsilon)
    normed_in = (tokens * inv_rms * norm_gain).astype(bf16)
    proj_scan = plain(normed_in, w_scan).astype(bf16)
    mixed_raw, mixer_back = jax.vjp(
        mixer_local,
        proj_scan[:, :CONV].astype(f32),
        proj_scan[:, CONV:].astype(f32),
        conv_weight,
        conv_bias,
        dt_bias,
        a_log,
        skip_gain,
    )
    gate_f = plain(normed_in, w_gate).astype(bf16).astype(f32)
    grad_out = cotangent[0]
    d_head = times_transposed(grad_out, w_out_full).astype(bf16).astype(f32)
    mixed_f = lax.optimization_barrier(mixed_raw.astype(bf16)).astype(f32)
    gate_sigmoid = jax.nn.sigmoid(gate_f)
    gate_silu = gate_f * gate_sigmoid
    gated_vals = mixed_f * gate_silu
    gate_rms = lax.rsqrt(jnp.mean(gated_vals * gated_vals, axis=1, keepdims=True) + epsilon)
    normed_out = (gated_vals * gate_rms * gate_gain).astype(bf16)
    d_w_out_part = over_rows(normed_out, grad_out)
    cross = jnp.mean(d_head * gate_gain * gated_vals, axis=1, keepdims=True)
    gain_grad = jnp.sum(d_head * gated_vals * gate_rms, axis=0)
    d_gated = gate_rms * gate_gain * d_head - gated_vals * gate_rms**3 * cross
    d_mixed = lax.optimization_barrier((d_gated * gate_silu).astype(bf16)).astype(f32)
    d_gate = (d_gated * mixed_f * gate_sigmoid * (1.0 + gate_f * (1.0 - gate_sigmoid))).astype(
        bf16
    )
    d_w_gate_part = over_rows(normed_in, d_gate)
    grad_w_out = reduced(d_w_out_part)
    grad_w_gate = reduced(d_w_gate_part)
    result = (tokens + plain(normed_out, w_out_full)).astype(bf16)
    d_xbc, d_step, conv_grad, bias_grad, shift_grad, decay_grad, skip_grad = mixer_back(d_mixed)
    d_scan = jnp.concatenate([d_xbc, d_step], axis=1).astype(bf16)
    grad_w_scan = reduced(over_rows(normed_in, d_scan))
    d_normed_in = times_transposed(d_gate, w_gate) + times_transposed(d_scan, w_scan)
    norm_gain_grad = jnp.sum(d_normed_in * tokens * inv_rms, axis=0)
    norm_cross = jnp.sum(d_normed_in * norm_gain * tokens, axis=1, keepdims=True)
    d_tokens = (
        inv_rms * norm_gain * d_normed_in
        - tokens * inv_rms**3 * norm_cross / D
        + grad_out.astype(f32)
    )
    small = (
        norm_gain_grad,
        conv_grad,
        bias_grad,
        shift_grad,
        decay_grad,
        skip_grad,
        gain_grad,
    )
    flat = lax.psum(jnp.concatenate([each.reshape(-1) for each in small]), ("seq", "fsdp"))
    sums, at = [], 0
    for each in small:
        sums.append(flat[at : at + each.size].reshape(each.shape))
        at += each.size
    return (
        result[None],
        d_tokens[None],
        sums[0],
        jnp.concatenate([grad_w_gate, grad_w_scan], axis=1),
        sums[1],
        sums[2],
        sums[3],
        sums[4],
        sums[5],
        sums[6],
        grad_w_out,
    )


def solution(mesh):
    rows = P("fsdp", None)
    part = P("fsdp", "seq", None)
    return jax.shard_map(
        body,
        mesh=mesh,
        in_specs=(part, P(), rows, P(), P(), P(), P(), P(), P(), rows, part),
        out_specs=(part, part, P(), rows, P(), P(), P(), P(), P(), P(), rows),
        check_vma=False,
    )
```

```python
from functools import partial

import jax
import jax.numpy as jnp
from jax import lax
from jax.sharding import PartitionSpec as P

D = 768
HEADS = 24
HEAD_DIM = 64
STATE = 128
CONVW = 4
CHUNK = 128
INNER = 1536
CONV = INNER + 2 * STATE

epsilon = 1e-05
precise = lax.Precision.HIGHEST
bf16 = jnp.bfloat16
f32 = jnp.float32


@partial(jax.custom_vjp, nondiff_argnums=(0,))
def mm(spec, left, right):
    return jnp.einsum(spec, left.astype(bf16), right.astype(bf16), preferred_element_type=f32)


def mm_keep(spec, left, right):
    left, right = left.astype(bf16), right.astype(bf16)
    return jnp.einsum(spec, left, right, preferred_element_type=f32), (left, right)


def mm_back(spec, kept, grad):
    left, right = kept
    sides, out = spec.split("->")
    one, two = sides.split(",")
    grad = grad.astype(bf16)
    return (
        jnp.einsum(f"{out},{two}->{one}", grad, right, preferred_element_type=f32),
        jnp.einsum(f"{one},{out}->{two}", left, grad, preferred_element_type=f32),
    )


mm.defvjp(mm_keep, mm_back)


def over_heads(values):
    spread = jnp.repeat(jnp.eye(HEADS, dtype=f32), HEAD_DIM, axis=1)
    return jnp.einsum("...h,hk->...k", values, spread, precision=precise)


def shifted(values, by):
    count = lax.axis_size("seq")
    return lax.ppermute(values, "seq", [(at, at + by) for at in range(count - by)])


def incoming(final_state, total):
    sent = final_state.astype(bf16)
    result = shifted(sent, 1).astype(f32)
    gap = 0.0
    for by in range(2, lax.axis_size("seq")):
        gap = gap + shifted(total, by - 1)
        result = result + over_heads(jnp.exp(gap))[None, :] * shifted(sent, by).astype(f32)
    return result


def state_scan(values, b_rows, c_rows, step_size, decay_rates):
    length = values.shape[0]
    chunks = length // CHUNK
    causal = jnp.arange(CHUNK)[:, None] >= jnp.arange(CHUNK)[None, :]
    x_c = values.reshape(chunks, CHUNK, INNER)
    b_c = b_rows.reshape(chunks, CHUNK, STATE)
    c_c = c_rows.reshape(chunks, CHUNK, STATE)
    dt_c = step_size.reshape(chunks, CHUNK, HEADS)
    decay_sum = jnp.einsum(
        "ts,csh->cth", causal.astype(f32), dt_c * decay_rates, precision=precise
    )
    total = decay_sum[:, -1, :]
    remain = jnp.exp(total[:, None, :] - decay_sum) * dt_c
    gains = mm("csn,csk->cnk", b_c, x_c * over_heads(remain))
    whole = over_heads(jnp.exp(total))
    starts = [jnp.zeros((STATE, INNER), f32)]
    for at in range(chunks):
        starts.append(starts[-1] * whole[at][None, :] + gains[at])
    first = incoming(starts[-1], jnp.sum(total, axis=0))
    before = over_heads(jnp.exp(jnp.cumsum(total, axis=0) - total))
    begun = jnp.stack(starts[:-1]) + before[:, None, :] * first[None]
    decay_cols = jnp.swapaxes(decay_sum, 1, 2)
    spread = jnp.where(
        causal[None, None], decay_cols[:, :, :, None] - decay_cols[:, :, None, :], 0.0
    )
    factor = jnp.where(causal[None, None], jnp.exp(spread), 0.0)
    crossing = mm("ctn,csn->cts", c_c, b_c)
    mixing = factor * crossing[:, None] * jnp.swapaxes(dt_c, 1, 2)[:, :, None, :]
    within = mm("chts,chsp->chtp", mixing, jnp.swapaxes(x_c.reshape(chunks, CHUNK, HEADS, HEAD_DIM), 1, 2))
    within = jnp.swapaxes(within, 1, 2).reshape(chunks, CHUNK, INNER)
    earlier = mm("ctn,cnk->ctk", c_c, begun) * over_heads(jnp.exp(decay_sum))
    return (within + earlier).reshape(length, INNER)


def mixer_local(xbc, raw_step, conv_weight, conv_bias, dt_bias, a_log, skip_gain):
    length = xbc.shape[0]
    halo = shifted(xbc[length - CONVW + 1 :].astype(bf16), 1).astype(f32)
    padded = jnp.concatenate([halo, xbc], axis=0)
    summed = conv_bias[None, :]
    for at in range(CONVW):
        summed = summed + conv_weight[at] * padded[at : at + length]
    filtered = jax.nn.silu(summed)
    step_size = jax.nn.softplus(raw_step + dt_bias)
    values = filtered[:, :INNER]
    scanned = state_scan(
        values,
        filtered[:, INNER : INNER + STATE],
        filtered[:, INNER + STATE :],
        step_size,
        -jnp.exp(a_log),
    )
    return scanned + over_heads(skip_gain)[None, :] * values


def plain(left_mat, right_mat):
    return jnp.dot(left_mat, right_mat, preferred_element_type=f32)


def times_transposed(left_mat, right_mat):
    return lax.dot_general(
        left_mat, right_mat, (((1,), (1,)), ((), ())), preferred_element_type=f32
    )


def over_rows(left_mat, right_mat):
    return lax.dot_general(
        left_mat, right_mat, (((0,), (0,)), ((), ())), preferred_element_type=f32
    )


def gathered(rows):
    return lax.all_gather(rows, "fsdp", axis=0, tiled=True)


def reduced(part):
    rows = lax.psum_scatter(part.astype(bf16), "fsdp", scatter_dimension=0, tiled=True)
    return lax.psum(rows, "seq").astype(f32)


def everywhere(values):
    for axis in ("fsdp", "seq"):
        count = lax.axis_size(axis)
        other = 1
        while other < count:
            values = values + lax.ppermute(values, axis, [(at, at ^ other) for at in range(count)])
            other *= 2
    return values


def body(
    hidden_in,
    norm_gain,
    w_in,
    conv_weight,
    conv_bias,
    dt_bias,
    a_log,
    skip_gain,
    gate_gain,
    w_out,
    cotangent,
):
    w_scan = gathered(w_in[:, INNER:])
    z_rows, o_rows, w_scan = lax.optimization_barrier((w_in[:, :INNER], w_out, w_scan))
    w_gate = gathered(z_rows)
    w_out_full = gathered(o_rows)
    tokens = hidden_in[0].astype(f32)
    inv_rms = lax.rsqrt(jnp.mean(tokens * tokens, axis=1, keepdims=True) + epsilon)
    normed_in = (tokens * inv_rms * norm_gain).astype(bf16)
    proj_scan = plain(normed_in, w_scan).astype(bf16)
    mixed_raw, mixer_back = jax.vjp(
        mixer_local,
        proj_scan[:, :CONV].astype(f32),
        proj_scan[:, CONV:].astype(f32),
        conv_weight,
        conv_bias,
        dt_bias,
        a_log,
        skip_gain,
    )
    gate_f = plain(normed_in, w_gate).astype(bf16).astype(f32)
    grad_out = cotangent[0]
    d_head = times_transposed(grad_out, w_out_full).astype(bf16).astype(f32)
    mixed_f = lax.optimization_barrier(mixed_raw.astype(bf16)).astype(f32)
    gate_sigmoid = jax.nn.sigmoid(gate_f)
    gate_silu = gate_f * gate_sigmoid
    gated_vals = mixed_f * gate_silu
    gate_rms = lax.rsqrt(jnp.mean(gated_vals * gated_vals, axis=1, keepdims=True) + epsilon)
    normed_out = (gated_vals * gate_rms * gate_gain).astype(bf16)
    d_w_out_part = over_rows(normed_out, grad_out)
    cross = jnp.mean(d_head * gate_gain * gated_vals, axis=1, keepdims=True)
    gain_grad = jnp.sum(d_head * gated_vals * gate_rms, axis=0)
    d_gated = gate_rms * gate_gain * d_head - gated_vals * gate_rms**3 * cross
    d_mixed = lax.optimization_barrier((d_gated * gate_silu).astype(bf16)).astype(f32)
    d_gate = (d_gated * mixed_f * gate_sigmoid * (1.0 + gate_f * (1.0 - gate_sigmoid))).astype(
        bf16
    )
    d_w_gate_part = over_rows(normed_in, d_gate)
    grad_w_out = reduced(d_w_out_part)
    grad_w_gate = reduced(d_w_gate_part)
    result = (tokens + plain(normed_out, w_out_full)).astype(bf16)
    d_xbc, d_step, conv_grad, bias_grad, shift_grad, decay_grad, skip_grad = mixer_back(d_mixed)
    d_scan = jnp.concatenate([d_xbc, d_step], axis=1).astype(bf16)
    grad_w_scan = reduced(over_rows(normed_in, d_scan))
    d_normed_in = times_transposed(d_gate, w_gate) + times_transposed(d_scan, w_scan)
    norm_gain_grad = jnp.sum(d_normed_in * tokens * inv_rms, axis=0)
    norm_cross = jnp.sum(d_normed_in * norm_gain * tokens, axis=1, keepdims=True)
    d_tokens = (
        inv_rms * norm_gain * d_normed_in
        - tokens * inv_rms**3 * norm_cross / D
        + grad_out.astype(f32)
    )
    small = (
        norm_gain_grad,
        conv_grad,
        bias_grad,
        shift_grad,
        decay_grad,
        skip_grad,
        gain_grad,
    )
    flat = everywhere(jnp.concatenate([each.reshape(-1) for each in small]))
    sums, at = [], 0
    for each in small:
        sums.append(flat[at : at + each.size].reshape(each.shape))
        at += each.size
    return (
        result[None],
        d_tokens[None],
        sums[0],
        jnp.concatenate([grad_w_gate, grad_w_scan], axis=1),
        sums[1],
        sums[2],
        sums[3],
        sums[4],
        sums[5],
        sums[6],
        grad_w_out,
    )


def solution(mesh):
    rows = P("fsdp", None)
    part = P("fsdp", "seq", None)
    return jax.shard_map(
        body,
        mesh=mesh,
        in_specs=(part, P(), rows, P(), P(), P(), P(), P(), P(), rows, part),
        out_specs=(part, part, P(), rows, P(), P(), P(), P(), P(), P(), rows),
        check_vma=False,
    )
```
